512 devices in a mesh: ops: 64 (over y_hi, z, core), blk: 8 (over x, y_lo).
Axes of the slice: x: 4, y: 8 (y_hi: 4, y_lo: 2; y = y_hi * 2 + y_lo), z: 8, core: 2. Of those that a mesh axis runs over, the one named last changes fastest.
Arguments:
- wave: float32 [384, 16, 384], P('ops', 'blk'), may hold values from -6 to 6
- left_op: float32 [128, 16, 384, 384], P('ops', 'blk'), may hold values from -1 to 13
- right_op: float32 [128, 16, 384, 384], P('ops', 'blk'), may hold values from -1 to 1
- left_dims: int32 [16], P('blk'), may hold values from 1 to 384, 2048 in all
- right_dims: int32 [16], P('blk'), may hold values from 1 to 384, 2048 in all
Outputs:
- sigma: float32 [384, 16, 384], P('ops', 'blk')
- residual: float32 [384, 16, 384], P('ops', 'blk')
The draws below stay inside these ranges and needn't reach their ends.
Inputs may be any that keep to these rules, and one draw needn't show every extreme that they name: `left_dims`: each sums to 2048; the largest is exactly 384. `right_dims`: each sums to 2048; the largest is exactly 384.
All inputs are finite; a program needn't handle non-finite values. No bound on the sum of `left_dims` or of `right_dims` on one device may be relied on, other than what follows from the above.
Results may differ from the reference program's by a relative error of at most 0.00029.
Values sent between devices are 32-bit elements; how exact they have to be, the bound alone decides.
A program may use at most 64 MiB of HBM per device.

```python
import math
import jax
import jax.numpy as jnp
import numpy as np
from jax import lax

MEAN = 128
CAP = 384
SECTORS = 16
TERMS = 128
BOND = 2048


def draw_left_op(key, part):
    key = jax.random.fold_in(key, 11)
    noise_key, factor_key, shift_key = jax.random.split(key, 3)
    noise = jax.random.truncated_normal(noise_key, -6.0, 6.0, (TERMS, SECTORS, CAP, CAP), jnp.float32) * MEAN ** (-0.5)
    factor = jnp.exp(jax.random.uniform(factor_key, (SECTORS,), jnp.float32, 0.0, math.log(4.0)))
    shift = jax.random.uniform(shift_key, (TERMS, SECTORS), jnp.float32, 0.5, 1.5)
    identity = jnp.eye(CAP, dtype=jnp.float32)
    return noise + (shift * factor[None, :])[:, :, None, None] * identity[None, None, :, :]


def draw_right_op(key, part):
    key = jax.random.fold_in(key, 23)
    noise_key, shift_key = jax.random.split(key, 2)
    noise = jax.random.truncated_normal(noise_key, -6.0, 6.0, (TERMS, SECTORS, CAP, CAP), jnp.float32) * (MEAN * TERMS) ** (-0.5)
    shift = jax.random.uniform(shift_key, (TERMS, SECTORS), jnp.float32, 0.5, 1.5)
    identity = jnp.eye(CAP, dtype=jnp.float32)
    return noise + (shift / TERMS)[:, :, None, None] * identity[None, None, :, :]


def shard_levels(stream_key, shape, cuts, least, top_value):
    level = 1.0
    for position, shards_of in cuts:
        heights = jax.random.uniform(jax.random.fold_in(jax.random.fold_in(stream_key, 6), position), (shards_of,), jnp.float32, least / len(cuts), top_value / len(cuts))
        level = level * jnp.repeat(jnp.exp(heights), shape[position] // shards_of).reshape((-1,) + (1,) * (len(shape) - 1 - position))
    return level


def profile(number_of, total, most, slope):
    portions = [(1 << 20) // math.isqrt(standing ** slope) + 1 for standing in range(2, number_of + 1)]
    rest, counts = total - most - (number_of - 1), [1] * (number_of - 1)
    while rest > 0:
        candidates = [i for i in range(number_of - 1) if counts[i] < most]
        pool, budget = sum([portions[i] for i in candidates]), rest
        for i in candidates:
            more = min(most - counts[i], max(1, budget * portions[i] // pool), rest)
            counts[i] = counts[i] + more
            rest = rest - more
    return np.array([most] + counts)


def ragged_sizes(rng, count, total, reach, slope):
    if count == 2:
        one = jax.random.randint(rng, (), max(1, total - reach), min(reach, total - 1) + 1)
        return jnp.stack([one, total - one])
    tallies = jnp.asarray(profile(count, total, reach, slope), jnp.int32)
    couples = (count - 1) // 2
    donor, sink = tallies[1:1 + 2 * couples:2], tallies[2:2 + 2 * couples:2]
    slack = jnp.minimum(donor - 1, reach - sink)
    passed = jax.random.randint(jax.random.fold_in(rng, 1), (couples,), 0, 1 << 20) % (slack + 1)
    tallies = tallies.at[1:1 + 2 * couples:2].set(donor - passed).at[2:2 + 2 * couples:2].set(sink + passed)
    return tallies[jax.random.permutation(jax.random.fold_in(rng, 2), count)]


def normal_values(key, shape, width, bound, pieces=(), kind=jnp.bfloat16):
    array = jax.random.normal(key, shape, jnp.float32) * width
    if len(pieces) > 0:
        array = shard_levels(key, shape, pieces, -0.22, 0.18) * array
    return jnp.clip(array, min=-bound, max=bound).astype(kind)


def setup_inputs(seed: int = 0) -> dict:
    streams_of = jax.random.split(jax.random.key(seed), 6)
    wave = normal_values(streams_of[0], (CAP, SECTORS, CAP), 1.0, 6.0, ((0, 64), (1, 8)), jnp.float32)
    left_op = draw_left_op(jax.random.fold_in(streams_of[5], 71), 0)
    right_op = draw_right_op(jax.random.fold_in(streams_of[5], 71), 0)
    left_dims = ragged_sizes(streams_of[3], SECTORS, BOND, CAP, 2).astype(jnp.int32)
    right_dims = ragged_sizes(streams_of[4], SECTORS, BOND, CAP, 2).astype(jnp.int32)
    return dict(wave=wave, left_op=left_op, right_op=right_op, left_dims=left_dims, right_dims=right_dims)


def sector_mask(left_dims, right_dims, offset, rows):
    row_ids = offset + jnp.arange(rows, dtype=jnp.int32)
    col_ids = jnp.arange(CAP, dtype=jnp.int32)
    inside = (row_ids[:, None, None] < left_dims[None, :, None]) & (col_ids[None, None, :] < right_dims[None, :, None])
    return inside.astype(jnp.float32)


def reference(wave, left_op, right_op, left_dims, right_dims):
    mask = sector_mask(left_dims, right_dims, jnp.int32(0), CAP)
    psi = wave * mask

    def add_term(total, pair):
        left_one, right_one = pair
        inner = jnp.einsum("sik,ksj->isj", left_one, psi, precision=lax.Precision.HIGHEST)
        return total + jnp.einsum("isk,sjk->isj", inner, right_one, precision=lax.Precision.HIGHEST), None

    total, unused = lax.scan(add_term, jnp.zeros(psi.shape, jnp.float32), (left_op, right_op))
    sigma = total * mask
    norm = jnp.sum(psi * psi)
    correlation = jnp.sum(psi * sigma)
    theta = correlation / norm
    residual = sigma - theta * psi
    return sigma, residual
```

```python
import jax
import jax.numpy as jnp
from jax import lax
from jax.experimental import pallas as pl
from jax.experimental.pallas import tpu as pltpu
from jax.sharding import PartitionSpec as P

Y, Z, C, B = 4, 8, 2, 8
ROWS = 6
CAP = 384
TERMS, SECT = 2, 2
MESH = pl.DeviceIdType.MESH
BF, F32 = jnp.bfloat16, jnp.float32


def split(x):
    high = x.astype(BF)
    return high, (x - high.astype(F32)).astype(BF)


def kernel(
    ld_ref, rd_ref, wave_ref, l_hbm, r_hbm, sigma_ref, resid_ref,
    lbuf, rbuf, load_sem,
    own, g0, g1, psi, la, pb, ra, rb, sig,
    s0, s1, t0, t1, u0, u1, v0, v1, w0, w1,
    q, qb, qc, qz, qy,
    ga_s, ga_r, gb_s, gb_r, gf_s, gf_r,
    rc_s, rc_r, ra_s, ra_r, rb_s, rb_r,
    q_s, q_r,
):
    o, b = lax.axis_index("ops"), lax.axis_index("blk")
    y, z, c = o // (Z * C), lax.rem(o // C, Z), lax.rem(o, C)
    other = 1 - c

    def dev(yy, zz, cc):
        return (yy * (Z * C) + zz * C + cc, b)

    def yplus(d):
        return lax.rem(y + d, Y)

    def zplus(d):
        return lax.rem(z + d, Z)

    def remote(src, dst, send, recv, to):
        return pltpu.make_async_remote_copy(
            src_ref=src, dst_ref=dst, send_sem=send, recv_sem=recv,
            device_id=to, device_id_type=MESH,
        )

    partner = dev(y, z, other)
    to_y = [None] + [dev(yplus(d), z, c) for d in range(1, Y)]
    to_z = [None] + [dev(y, zplus(d), c) for d in range(1, Z)]
    to_b = [None] + [(o, lax.rem(b + d, B)) for d in range(1, B)]
    peers = to_y[1:] + to_z[1:] + to_b[1:] + [partner]

    barrier = pltpu.get_barrier_semaphore()
    for to in peers:
        pl.semaphore_signal(barrier, inc=1, device_id=to, device_id_type=MESH)

    loads = []
    for s in range(SECT):
        for t in range(TERMS):
            loads.append((
                pltpu.make_async_copy(l_hbm.at[t, s], lbuf.at[t, s], load_sem.at[0, t, s]),
                pltpu.make_async_copy(r_hbm.at[t, s], rbuf.at[t, s], load_sem.at[1, t, s]),
            ))
    for one, two in loads:
        one.start()
        two.start()

    row_ids = o * ROWS + lax.broadcasted_iota(jnp.int32, (ROWS, CAP), 0)
    col_ids = lax.broadcasted_iota(jnp.int32, (ROWS, CAP), 1)
    masks = []
    for s in range(SECT):
        masks.append(
            ((row_ids < ld_ref[s]) & (col_ids < rd_ref[s])).astype(F32)
        )
        for i in range(ROWS):
            own[s, i : i + 1, :] = wave_ref[i, s : s + 1, :]
        own[s] = own[s] * masks[s]
    g0[z, c, y] = own[0]
    g1[y, c, z] = own[1]
    square = own[0] * own[0] + own[1] * own[1]
    q[...] = jnp.zeros_like(q)
    q[1, 0:ROWS, :] = sum(square[:, k : k + 128] for k in range(0, CAP, 128))

    pl.semaphore_wait(barrier, len(peers))

    sends = []

    def go(copy):
        copy.start()
        sends.append(copy)

    for d in range(1, Z):
        slot = g1.at[y, c, z]
        go(remote(slot, slot, ga_s.at[d], ga_r.at[d], to_z[d]))
    for d in range(1, Y):
        slot = g0.at[z, c, y]
        go(remote(slot, slot, ga_s.at[Z + d], ga_r.at[Z + d], to_y[d]))

    def prepare_left(s):
        for t in range(TERMS):
            loads[s * TERMS + t][0].wait()
            high, low = split(lbuf[t, s])
            rows = pl.ds(t * CAP, CAP)
            la[s, rows, 0:CAP] = high
            la[s, rows, CAP : 2 * CAP] = high
            la[s, rows, 2 * CAP : 3 * CAP] = low

    def prepare_right(s):
        for t in range(TERMS):
            loads[s * TERMS + t][1].wait()
            high, low = split(jnp.transpose(rbuf[t, s]))
            at = 3 * CAP * t
            rb[s, at : at + CAP, :] = high
            rb[s, at + CAP : at + 2 * CAP, :] = low
            rb[s, at + 2 * CAP : at + 3 * CAP, :] = high

    for d in range(1, Y):
        slot = g0.at[z, c, lax.rem(y - d + Y, Y)]
        remote(slot, slot, ga_s.at[Z + d], ga_r.at[Z + d], to_y[d]).wait_recv()
    bundle = g0.at[z, c]
    for d in range(1, Z):
        go(remote(bundle, bundle, gb_s.at[d], gb_r.at[d], to_z[d]))
    go(remote(bundle, bundle, gf_s.at[0], gf_r.at[0], partner))
    for d in range(1, Z):
        slot = g1.at[y, c, lax.rem(z - d + Z, Z)]
        remote(slot, slot, ga_s.at[d], ga_r.at[d], to_z[d]).wait_recv()
    bundle = g1.at[y, c]
    for d in range(1, Y):
        go(remote(bundle, bundle, gb_s.at[Z + d], gb_r.at[Z + d], to_y[d]))
    go(remote(bundle, bundle, gf_s.at[Z], gf_r.at[Z], partner))

    for s in range(SECT):
        prepare_left(s)
        prepare_right(s)

    for d in sorted(range(1, Z), key=lambda d: min(d, Z - d)):
        slot = g0.at[lax.rem(z - d + Z, Z), c]
        remote(slot, slot, gb_s.at[d], gb_r.at[d], to_z[d]).wait_recv()
        go(remote(slot, slot, gf_s.at[d], gf_r.at[d], partner))
    for d in sorted(range(1, Y), key=lambda d: min(d, Y - d)):
        slot = g1.at[lax.rem(y - d + Y, Y), c]
        remote(slot, slot, gb_s.at[Z + d], gb_r.at[Z + d], to_y[d]).wait_recv()
        go(remote(slot, slot, gf_s.at[Z + d], gf_r.at[Z + d], partner))

    def unpack(s):
        def body(g, carry):
            yy, zp = g // (Z // 2), lax.rem(g, Z // 2)
            parts = []
            for k in range(4):
                zz, cc = 2 * zp + k // 2, k % 2
                parts.append(g0[zz, cc, yy] if s == 0 else g1[yy, cc, zz])
            at = pl.multiple_of(g * 4 * ROWS, 8)
            psi[s, pl.ds(at, 4 * ROWS), :] = jnp.concatenate(parts, axis=0)
            return carry

        lax.fori_loop(0, Y * Z // 2, body, 0)
        high, low = split(psi[s])
        pb[s, 0:CAP, :] = high
        pb[s, CAP : 2 * CAP, :] = low
        pb[s, 2 * CAP : 3 * CAP, :] = high

    def products(s):
        inner = jnp.dot(la[s], pb[s], preferred_element_type=F32)
        for t in range(TERMS):
            high, low = split(inner[t * CAP : (t + 1) * CAP])
            at = 3 * CAP * t
            ra[s, :, at : at + CAP] = high
            ra[s, :, at + CAP : at + 2 * CAP] = high
            ra[s, :, at + 2 * CAP : at + 3 * CAP] = low
        sig[s] = jnp.dot(ra[s], rb[s], preferred_element_type=F32)

    def pack(s):
        def body(g, total):
            yy, zp = g // (Z // 2), lax.rem(g, Z // 2)
            at = pl.multiple_of(g * 4 * ROWS, 8)
            block = sig[s, pl.ds(at, 4 * ROWS), :]
            pair = block * psi[s, pl.ds(at, 4 * ROWS), :]
            for i in range(0, 4 * ROWS, 8):
                for j in range(0, CAP, 128):
                    total = total + pair[i : i + 8, j : j + 128]
            for k in range(4):
                zz, cc = 2 * zp + k // 2, k % 2
                part = block[k * ROWS : (k + 1) * ROWS]
                if s == 0:
                    s0[cc, zz, yy] = part
                else:
                    s1[cc, yy, zz] = part
            return total

        return lax.fori_loop(0, Y * Z // 2, body, jnp.zeros((8, 128), F32))

    core = []
    total = None
    for s in range(SECT):
        if s == 0:
            for d in range(Z):
                slot = g0.at[lax.rem(z - d + Z, Z), other]
                remote(slot, slot, gf_s.at[d], gf_r.at[d], partner).wait_recv()
        else:
            for d in range(Y):
                slot = g1.at[lax.rem(y - d + Y, Y), other]
                remote(slot, slot, gf_s.at[Z + d], gf_r.at[Z + d], partner).wait_recv()
        unpack(s)
        products(s)
        part = pack(s)
        total = part if total is None else total + part
        src, dst = ((s0, t0), (s1, t1))[s]
        copy = remote(src.at[other], dst, rc_s.at[s], rc_r.at[s], partner)
        go(copy)
        core.append(copy)
    q[0] = total

    for d in range(1, B):
        go(remote(q, qb.at[d], q_s.at[d], q_r.at[d], to_b[d]))

    core[0].wait_recv()
    order_z = sorted(range(1, Z), key=lambda d: -min(d, Z - d))
    order_y = sorted(range(1, Y), key=lambda d: -min(d, Y - d))
    for d in order_z + [0]:
        zz = zplus(d)
        s0[c, zz] = s0[c, zz] + t0[zz]
        if d:
            go(remote(s0.at[c, zz], u0.at[d], ra_s.at[d], ra_r.at[d], to_z[d]))
    core[1].wait_recv()
    for d in order_y + [0]:
        yy = yplus(d)
        s1[c, yy] = s1[c, yy] + t1[yy]
        if d:
            go(remote(s1.at[c, yy], u1.at[d], ra_s.at[Z + d], ra_r.at[Z + d], to_y[d]))

    acc = q[...]
    for d in range(1, B):
        remote(q, qb.at[d], q_s.at[d], q_r.at[d], to_b[d]).wait_recv()
        acc = acc + qb[d]
    qb[0] = acc
    copy = remote(qb.at[0], qc.at[1], q_s.at[0], q_r.at[0], partner)
    go(copy)
    copy.wait_recv()
    acc = acc + qc[1]
    qc[0] = acc
    for d in range(1, Z):
        go(remote(qc.at[0], qz.at[d], q_s.at[B + d], q_r.at[B + d], to_z[d]))
    for d in range(1, Z):
        remote(qc.at[0], qz.at[d], q_s.at[B + d], q_r.at[B + d], to_z[d]).wait_recv()
        acc = acc + qz[d]
    qz[0] = acc
    for d in range(1, Y):
        go(remote(qz.at[0], qy.at[d], q_s.at[B + Z + d], q_r.at[B + Z + d], to_y[d]))

    tot = s0[c, z]
    for d in reversed(order_z):
        remote(s0.at[c, z], u0.at[d], ra_s.at[d], ra_r.at[d], to_z[d]).wait_recv()
        tot = tot + u0[d]
    v0[...] = tot
    for d in order_y:
        go(remote(v0.at[yplus(d)], w0.at[d], rb_s.at[Z + d], rb_r.at[Z + d], to_y[d]))
    tot = s1[c, y]
    for d in reversed(order_y):
        remote(s1.at[c, y], u1.at[d], ra_s.at[Z + d], ra_r.at[Z + d], to_y[d]).wait_recv()
        tot = tot + u1[d]
    v1[...] = tot
    for d in order_z:
        go(remote(v1.at[zplus(d)], w1.at[d], rb_s.at[d], rb_r.at[d], to_z[d]))

    for d in range(1, Y):
        remote(qz.at[0], qy.at[d], q_s.at[B + Z + d], q_r.at[B + Z + d], to_y[d]).wait_recv()
        acc = acc + qy[d]
    theta = jnp.sum(acc[0], keepdims=True) / jnp.sum(acc[1], keepdims=True)

    out0 = v0[y]
    for d in range(1, Y):
        remote(v0.at[y], w0.at[d], rb_s.at[Z + d], rb_r.at[Z + d], to_y[d]).wait_recv()
        out0 = out0 + w0[d]
    out1 = v1[z]
    for d in range(1, Z):
        remote(v1.at[z], w1.at[d], rb_s.at[d], rb_r.at[d], to_z[d]).wait_recv()
        out1 = out1 + w1[d]
    for s, out in ((0, out0), (1, out1)):
        out = out * masks[s]
        res = out - theta * own[s]
        for i in range(ROWS):
            sigma_ref[i, s : s + 1, :] = out[i : i + 1]
            resid_ref[i, s : s + 1, :] = res[i : i + 1]
    for copy in sends:
        copy.wait_send()


def local(wave, left_op, right_op, left_dims, right_dims):
    dma = pltpu.SemaphoreType.DMA
    chunk = (ROWS, CAP)
    vmem, smem = pltpu.VMEM, pltpu.SMEM
    return pl.pallas_call(
        kernel,
        out_shape=[jax.ShapeDtypeStruct((ROWS, SECT, CAP), F32)] * 2,
        in_specs=[
            pl.BlockSpec(memory_space=smem),
            pl.BlockSpec(memory_space=smem),
            pl.BlockSpec(memory_space=vmem),
            pl.BlockSpec(memory_space=pl.ANY),
            pl.BlockSpec(memory_space=pl.ANY),
        ],
        out_specs=[pl.BlockSpec(memory_space=vmem)] * 2,
        scratch_shapes=[
            vmem((TERMS, SECT, CAP, CAP), F32),
            vmem((TERMS, SECT, CAP, CAP), F32),
            dma((2, TERMS, SECT)),
            vmem((SECT,) + chunk, F32),
            vmem((Z, C, Y) + chunk, F32),
            vmem((Y, C, Z) + chunk, F32),
            vmem((SECT, CAP, CAP), F32),
            vmem((SECT, TERMS * CAP, 3 * CAP), BF),
            vmem((SECT, 3 * CAP, CAP), BF),
            vmem((SECT, CAP, 3 * TERMS * CAP), BF),
            vmem((SECT, 3 * TERMS * CAP, CAP), BF),
            vmem((SECT, CAP, CAP), F32),
            vmem((C, Z, Y) + chunk, F32),
            vmem((C, Y, Z) + chunk, F32),
            vmem((Z, Y) + chunk, F32),
            vmem((Y, Z) + chunk, F32),
            vmem((Z, Y) + chunk, F32),
            vmem((Y, Z) + chunk, F32),
            vmem((Y,) + chunk, F32),
            vmem((Z,) + chunk, F32),
            vmem((Y,) + chunk, F32),
            vmem((Z,) + chunk, F32),
            vmem((2, 8, 128), F32),
            vmem((B, 2, 8, 128), F32),
            vmem((2, 2, 8, 128), F32),
            vmem((Z, 2, 8, 128), F32),
            vmem((Y, 2, 8, 128), F32),
        ]
        + [dma((Z + Y,))] * 6
        + [dma((SECT,))] * 2
        + [dma((Z + Y,))] * 4
        + [dma((B + Z + Y,))] * 2,
        compiler_params=pltpu.CompilerParams(
            collective_id=0, has_side_effects=True, vmem_limit_bytes=48 * 1024 * 1024
        ),
        cost_estimate=pl.CostEstimate(
            flops=6_000_000_000, bytes_accessed=5_000_000, transcendentals=0
        ),
    )(left_dims, right_dims, wave, left_op, right_op)


def solution(mesh):
    in_specs = (
        P("ops", "blk", None),
        P("ops", "blk", None, None),
        P("ops", "blk", None, None),
        P("blk"),
        P("blk"),
    )
    out_specs = (P("ops", "blk", None), P("ops", "blk", None))
    return jax.shard_map(local, mesh=mesh, in_specs=in_specs, out_specs=out_specs, check_vma=False)
```

```python
import jax
import jax.numpy as jnp
from jax import lax
from jax.experimental import pallas as pl
from jax.experimental.pallas import tpu as pltpu
from jax.sharding import PartitionSpec as P

Y, Z, C, B = 4, 8, 2, 8
ROWS = 6
CAP = 384
TERMS, SECT = 2, 2
MESH = pl.DeviceIdType.MESH
BF, F32 = jnp.bfloat16, jnp.float32


def split(x):
    high = x.astype(BF)
    return high, (x - high.astype(F32)).astype(BF)


def kernel(
    ld_hbm, rd_hbm, wave_hbm, l_hbm, r_hbm, sigma_ref, resid_ref,
    ld_ref, rd_ref, wave_ref, in_sem,
    lbuf, rbuf, load_sem,
    own, near, ga, gb, psi, la, pb, ra, rb, sig,
    sa, sb, ta, tb, ua, ub, vl, wl, fin,
    q, qb, qh, ql,
    li_s, li_r, hi_s, hi_r, fa_s, fa_r, fb_s, fb_r,
    co_s, co_r, ho_s, ho_r, lo_s, lo_r,
    qb_s, qb_r, qh_s, qh_r, ql_s, ql_r,
):
    small = [
        pltpu.make_async_copy(wave_hbm, wave_ref, in_sem.at[0]),
        pltpu.make_async_copy(ld_hbm, ld_ref, in_sem.at[1]),
        pltpu.make_async_copy(rd_hbm, rd_ref, in_sem.at[2]),
    ]
    for copy in small:
        copy.start()

    o, b = lax.axis_index("ops"), lax.axis_index("blk")
    y, z, c = o // (Z * C), lax.rem(o // C, Z), lax.rem(o, C)
    other = 1 - c
    yp = [lax.rem(y + d, Y) for d in range(Y)]
    ym = [lax.rem(y - d + Y, Y) for d in range(Y)]
    zp = [lax.rem(z + d, Z) for d in range(Z)]
    zm = [lax.rem(z - d + Z, Z) for d in range(Z)]

    def dev(yy, zz, cc, bb):
        return (yy * (Z * C) + zz * C + cc, bb)

    def remote(src, dst, send, recv, to):
        return pltpu.make_async_remote_copy(
            src_ref=src, dst_ref=dst, send_sem=send, recv_sem=recv,
            device_id=to, device_id_type=MESH,
        )

    partner = dev(y, z, other, b)
    to_y = [dev(yp[d], z, c, b) for d in range(Y)]
    to_z = [dev(y, zp[d], c, b) for d in range(Z)]
    to_b = [
        dev(y, z, other if k % 2 else c, lax.rem(b + k // 2, B)) for k in range(2 * B)
    ]
    peers = to_y[1:] + to_z[1:] + to_b[1:]

    barrier = pltpu.get_barrier_semaphore()
    for to in peers:
        pl.semaphore_signal(barrier, inc=1, device_id=to, device_id_type=MESH)

    loads = [
        [
            (
                pltpu.make_async_copy(l_hbm.at[t, s], lbuf.at[t, s], load_sem.at[0, t, s]),
                pltpu.make_async_copy(r_hbm.at[t, s], rbuf.at[t, s], load_sem.at[1, t, s]),
            )
            for t in range(TERMS)
        ]
        for s in range(SECT)
    ]
    for s in range(SECT):
        for t in range(TERMS):
            loads[s][t][0].start()
            loads[s][t][1].start()

    row_ids = o * ROWS + lax.broadcasted_iota(jnp.int32, (ROWS, CAP), 0)
    col_ids = lax.broadcasted_iota(jnp.int32, (ROWS, CAP), 1)
    for copy in small:
        copy.wait()
    masks = []
    me = y * other + z * c
    for s in range(SECT):
        masks.append(
            ((row_ids < ld_ref[s]) & (col_ids < rd_ref[s])).astype(F32)
        )
        for i in range(ROWS):
            own[s, i : i + 1, :] = wave_ref[i, s : s + 1, :]
        own[s] = own[s] * masks[s]
        near[me, s] = own[s]

    pl.semaphore_wait(barrier, len(peers))

    class Path:
        pass

    one, two = Path(), Path()
    one.light, one.heavy, one.light_m, one.heavy_m = to_y, to_z, ym, zm
    one.light_p, one.heavy_p = yp, zp
    one.light_me, one.heavy_me = y, z
    one.g, one.s, one.t, one.u, one.f_s, one.f_r = ga, sa, ta, ua, fa_s, fa_r
    two.light, two.heavy, two.light_m, two.heavy_m = to_z, to_y, zm, ym
    two.light_p, two.heavy_p = zp, yp
    two.light_me, two.heavy_me = z, y
    two.g, two.s, two.t, two.u, two.f_s, two.f_r = gb, sb, tb, ub, fb_s, fb_r
    for p, o_ in ((one, two), (two, one)):
        p.other = o_
        p.n, p.m = len(p.light), len(p.heavy)
        p.near_first = sorted(range(1, p.m), key=lambda d: min(d, p.m - d))
        p.far_first = p.near_first[::-1]
    sends = []

    def both(step, *args):
        @pl.when(c == 0)
        def _():
            step(one, *args)

        @pl.when(c == 1)
        def _():
            step(two, *args)

    def go(copy):
        copy.start()

    def gather_start(p):
        slot = near.at[p.light_me]
        for d in range(1, p.n):
            go(remote(slot, slot, li_s.at[d], li_r.at[d], p.light[d]))
        for d in range(1, p.n):
            slot = near.at[p.light_m[d]]
            remote(slot, slot, li_s.at[d], li_r.at[d], p.light[d]).wait_recv()
        for s in range(SECT):
            for k in range(p.n):
                p.g[s, p.heavy_me, k * ROWS : (k + 1) * ROWS, :] = near[k, s]
            slot = p.g.at[s, p.heavy_me]
            for d in p.far_first:
                go(remote(slot, slot, hi_s.at[s, d], hi_r.at[s, d], p.heavy[d]))
            go(remote(slot, slot, p.f_s.at[s, 0], p.f_r.at[s, 0], partner))

    def gather_forward(p, s):
        for d in p.near_first:
            slot = p.g.at[s, p.heavy_m[d]]
            remote(slot, slot, hi_s.at[s, d], hi_r.at[s, d], p.heavy[d]).wait_recv()
            go(remote(slot, slot, p.f_s.at[s, d], p.f_r.at[s, d], partner))

    def gather_finish(p, s):
        p = p.other
        for d in range(p.m):
            slot = p.g.at[s, p.heavy_m[d]]
            remote(slot, slot, p.f_s.at[s, d], p.f_r.at[s, d], partner).wait_recv()

    def prepare(s):
        for t in range(TERMS):
            loads[s][t][0].wait()
            high, low = split(lbuf[t, s])
            rows = pl.ds(t * CAP, CAP)
            la[s, rows, 0:CAP] = high
            la[s, rows, CAP : 2 * CAP] = high
            la[s, rows, 2 * CAP : 3 * CAP] = low
        for t in range(TERMS):
            loads[s][t][1].wait()
            high, low = split(jnp.transpose(rbuf[t, s]))
            at = 3 * CAP * t
            rb[s, at : at + CAP, :] = high
            rb[s, at + CAP : at + 2 * CAP, :] = low
            rb[s, at + 2 * CAP : at + 3 * CAP, :] = high

    def unpack(s):
        for g in range(Y * Z // 4):
            yy = g // 2
            parts = []
            for zz in range(4 * (g % 2), 4 * (g % 2) + 4):
                parts.append(ga[s, zz, yy * ROWS : (yy + 1) * ROWS, :])
                parts.append(gb[s, yy, zz * ROWS : (zz + 1) * ROWS, :])
            block = jnp.concatenate(parts, axis=0)
            at, n = g * 8 * ROWS, 8 * ROWS
            psi[s, at : at + n, :] = block
            high, low = split(block)
            pb[s, at : at + n, :] = high
            pb[s, CAP + at : CAP + at + n, :] = low
            pb[s, 2 * CAP + at : 2 * CAP + at + n, :] = high

    def first_product(s):
        inner = jnp.dot(la[s], pb[s], preferred_element_type=F32)
        for t in range(TERMS):
            high, low = split(inner[t * CAP : (t + 1) * CAP])
            at = 3 * CAP * t
            ra[s, :, at : at + CAP] = high
            ra[s, :, at + CAP : at + 2 * CAP] = high
            ra[s, :, at + 2 * CAP : at + 3 * CAP] = low

    def second_product(s):
        sig[s] = jnp.dot(ra[s], rb[s], preferred_element_type=F32)

    def pack(s):
        for g in range(Y * Z // 2):
            yy = g // 4
            at, n = g * 4 * ROWS, 4 * ROWS
            block = sig[s, at : at + n, :]
            for k in range(4):
                zz, cc = 2 * (g % 4) + k // 2, k % 2
                part = block[k * ROWS : (k + 1) * ROWS]
                if cc == 0:
                    sa[s, zz, yy * ROWS : (yy + 1) * ROWS, :] = part
                else:
                    sb[s, yy, zz * ROWS : (zz + 1) * ROWS, :] = part

    def core_start(p, s):
        r = p.other
        go(remote(r.s.at[s], r.t.at[s], co_s.at[s], co_r.at[s], partner))

    def correlate(s):
        def body(i, total):
            rows = pl.ds(pl.multiple_of(i * 16, 16), 16)
            pair = sig[s, rows, :] * psi[s, rows, :]
            for i in (0, 8):
                for j in range(0, CAP, 128):
                    total = total + pair[i : i + 8, j : j + 128]
            return total

        return lax.fori_loop(0, CAP // 16, body, jnp.zeros((8, 128), F32))

    def scatter_start(p, s):
        remote(p.s.at[s], p.t.at[s], co_s.at[s], co_r.at[s], partner).wait_recv()
        for d in p.far_first + [0]:
            at = p.heavy_p[d]
            p.s[s, at] = p.s[s, at] + p.t[s, at]
            if d:
                go(remote(p.s.at[s, at], p.u.at[s, d], ho_s.at[s, d], ho_r.at[s, d], p.heavy[d]))

    def scalars_start(p):
        for d in p.far_first:
            go(remote(qh.at[0], qh.at[d], qh_s.at[d], qh_r.at[d], p.heavy[d]))

    def scatter_sum(p, s):
        total = p.s[s, p.heavy_me]
        for d in p.near_first:
            remote(p.s.at[s, 0], p.u.at[s, d], ho_s.at[s, d], ho_r.at[s, d], p.heavy[d]).wait_recv()
            total = total + p.u[s, d]
        for k in range(p.n):
            vl[k, s] = total[k * ROWS : (k + 1) * ROWS]

    def scatter_finish(p):
        order = sorted(range(1, p.n), key=lambda d: -min(d, p.n - d))
        for d in order:
            go(remote(vl.at[p.light_p[d]], wl.at[d], lo_s.at[d], lo_r.at[d], p.light[d]))
        total = qh[0]
        for d in range(1, p.m):
            remote(qh.at[0], qh.at[d], qh_s.at[d], qh_r.at[d], p.heavy[d]).wait_recv()
            total = total + qh[d]
        ql[0] = total
        for d in order:
            go(remote(ql.at[0], ql.at[d], ql_s.at[d], ql_r.at[d], p.light[d]))
        out = vl[p.light_me]
        for d in order[::-1]:
            remote(vl.at[0], wl.at[d], lo_s.at[d], lo_r.at[d], p.light[d]).wait_recv()
            out = out + wl[d]
        fin[...] = out
        for d in order[::-1]:
            remote(ql.at[0], ql.at[d], ql_s.at[d], ql_r.at[d], p.light[d]).wait_recv()
            total = total + ql[d]
        q[...] = total

    both(gather_start)
    square = own[0] * own[0] + own[1] * own[1]
    q[...] = jnp.zeros_like(q)
    q[1, 0:ROWS, :] = sum(square[:, k : k + 128] for k in range(0, CAP, 128))
    for s in range(SECT):
        prepare(s)
    both(gather_forward, 0)
    both(gather_finish, 0)
    unpack(0)
    first_product(0)
    both(gather_forward, 1)
    second_product(0)
    pack(0)
    both(core_start, 0)
    both(gather_finish, 1)
    unpack(1)
    first_product(1)
    both(scatter_start, 0)
    second_product(1)
    pack(1)
    both(core_start, 1)
    q[0] = correlate(0) + correlate(1)
    for k in range(1, 2 * B):
        copy = remote(q, qb.at[k], qb_s.at[k], qb_r.at[k], to_b[k])
        copy.start()
        sends.append(copy)
    both(scatter_start, 1)
    total = q[...]
    for k in range(1, 2 * B):
        remote(q, qb.at[k], qb_s.at[k], qb_r.at[k], to_b[k]).wait_recv()
        total = total + qb[k]
    qh[0] = total
    for copy in sends:
        copy.wait_send()
    both(scalars_start)
    both(scatter_sum, 0)
    both(scatter_sum, 1)
    both(scatter_finish)

    theta = jnp.sum(q[0], keepdims=True) / jnp.sum(q[1], keepdims=True)
    for s in range(SECT):
        out = fin[s] * masks[s]
        res = out - theta * own[s]
        for i in range(ROWS):
            sigma_ref[i, s : s + 1, :] = out[i : i + 1]
            resid_ref[i, s : s + 1, :] = res[i : i + 1]

    def finish(p):
        for d in range(1, p.n):
            remote(near.at[0], near.at[0], li_s.at[d], li_r.at[d], partner).wait_send()
            remote(vl.at[0], wl.at[d], lo_s.at[d], lo_r.at[d], partner).wait_send()
            remote(ql.at[0], ql.at[d], ql_s.at[d], ql_r.at[d], partner).wait_send()
        for d in range(1, p.m):
            remote(qh.at[0], qh.at[d], qh_s.at[d], qh_r.at[d], partner).wait_send()
        for s in range(SECT):
            slot, r = p.g.at[s, 0], p.other
            for d in range(p.m):
                remote(slot, slot, p.f_s.at[s, d], p.f_r.at[s, d], partner).wait_send()
            for d in range(1, p.m):
                remote(slot, slot, hi_s.at[s, d], hi_r.at[s, d], partner).wait_send()
                remote(p.s.at[s, 0], p.u.at[s, d], ho_s.at[s, d], ho_r.at[s, d], partner).wait_send()
            remote(r.s.at[s], r.t.at[s], co_s.at[s], co_r.at[s], partner).wait_send()

    both(finish)


def local(wave, left_op, right_op, left_dims, right_dims):
    dma = pltpu.SemaphoreType.DMA
    chunk = (ROWS, CAP)
    vmem, smem = pltpu.VMEM, pltpu.SMEM
    return pl.pallas_call(
        kernel,
        out_shape=[jax.ShapeDtypeStruct((ROWS, SECT, CAP), F32)] * 2,
        in_specs=[pl.BlockSpec(memory_space=pltpu.HBM)] * 5,
        out_specs=[pl.BlockSpec(memory_space=vmem)] * 2,
        scratch_shapes=[
            smem((SECT,), jnp.int32),
            smem((SECT,), jnp.int32),
            vmem((ROWS, SECT, CAP), F32),
            dma((3,)),
            vmem((TERMS, SECT, CAP, CAP), F32),
            vmem((TERMS, SECT, CAP, CAP), F32),
            dma((2, TERMS, SECT)),
            vmem((SECT,) + chunk, F32),
            vmem((Z, SECT) + chunk, F32),
            vmem((SECT, Z, Y * ROWS, CAP), F32),
            vmem((SECT, Y, Z * ROWS, CAP), F32),
            vmem((SECT, CAP, CAP), F32),
            vmem((SECT, TERMS * CAP, 3 * CAP), BF),
            vmem((SECT, 3 * CAP, CAP), BF),
            vmem((SECT, CAP, 3 * TERMS * CAP), BF),
            vmem((SECT, 3 * TERMS * CAP, CAP), BF),
            vmem((SECT, CAP, CAP), F32),
        ]
        + [vmem((SECT, Z, Y * ROWS, CAP), F32), vmem((SECT, Y, Z * ROWS, CAP), F32)] * 3
        + [
            vmem((Z, SECT) + chunk, F32),
            vmem((Z, SECT) + chunk, F32),
            vmem((SECT,) + chunk, F32),
            vmem((2, 8, 128), F32),
            vmem((2 * B, 2, 8, 128), F32),
            vmem((Z, 2, 8, 128), F32),
            vmem((Z, 2, 8, 128), F32),
        ]
        + [dma((Z,))] * 2
        + [dma((SECT, Z))] * 6
        + [dma((SECT,))] * 2
        + [dma((SECT, Z))] * 2
        + [dma((Z,))] * 2
        + [dma((2 * B,))] * 2
        + [dma((Z,))] * 4,
        compiler_params=pltpu.CompilerParams(
            collective_id=0, has_side_effects=True, vmem_limit_bytes=64 * 1024 * 1024
        ),
        cost_estimate=pl.CostEstimate(
            flops=6_000_000_000, bytes_accessed=5_000_000, transcendentals=0
        ),
    )(left_dims, right_dims, wave, left_op, right_op)


def solution(mesh):
    in_specs = (
        P("ops", "blk", None),
        P("ops", "blk", None, None),
        P("ops", "blk", None, None),
        P("blk"),
        P("blk"),
    )
    out_specs = (P("ops", "blk", None), P("ops", "blk", None))
    return jax.shard_map(local, mesh=mesh, in_specs=in_specs, out_specs=out_specs, check_vma=False)
```

```python
import jax
import jax.numpy as jnp
from jax import lax
from jax.experimental import pallas as pl
from jax.experimental.pallas import tpu as pltpu
from jax.sharding import PartitionSpec as P

Y, Z, C, B = 4, 8, 2, 8
ROWS = 6
CAP = 384
TERMS, SECT = 2, 2
MESH = pl.DeviceIdType.MESH
BF, F32 = jnp.bfloat16, jnp.float32


def split(x):
    high = x.astype(BF)
    return high, (x - high.astype(F32)).astype(BF)


def kernel(
    ld_hbm, rd_hbm, wave_hbm, l_hbm, r_hbm, raw_ref, mask_ref, shift_ref,
    ld_ref, rd_ref, wave_ref, in_sem,
    lbuf, rbuf, load_sem,
    own, near, ga, gb, psi, la, pb, ra, rb, sig,
    sa, sb, ta, tb, ua, ub, vl, wl, fin,
    q, qb, qh, ql,
    li_s, li_r, hi_s, hi_r, fa_s, fa_r, fb_s, fb_r,
    co_s, co_r, ho_s, ho_r, lo_s, lo_r,
    qb_s, qb_r, qh_s, qh_r, ql_s, ql_r,
):
    small = [
        pltpu.make_async_copy(wave_hbm, wave_ref, in_sem.at[0]),
        pltpu.make_async_copy(ld_hbm, ld_ref, in_sem.at[1]),
        pltpu.make_async_copy(rd_hbm, rd_ref, in_sem.at[2]),
    ]
    for copy in small:
        copy.start()

    o, b = lax.axis_index("ops"), lax.axis_index("blk")
    y, z, c = o // (Z * C), lax.rem(o // C, Z), lax.rem(o, C)
    other = 1 - c
    yp = [lax.rem(y + d, Y) for d in range(Y)]
    ym = [lax.rem(y - d + Y, Y) for d in range(Y)]
    zp = [lax.rem(z + d, Z) for d in range(Z)]
    zm = [lax.rem(z - d + Z, Z) for d in range(Z)]

    def dev(yy, zz, cc, bb):
        return (yy * (Z * C) + zz * C + cc, bb)

    def remote(src, dst, send, recv, to):
        return pltpu.make_async_remote_copy(
            src_ref=src, dst_ref=dst, send_sem=send, recv_sem=recv,
            device_id=to, device_id_type=MESH,
        )

    partner = dev(y, z, other, b)
    to_y = [dev(yp[d], z, c, b) for d in range(Y)]
    to_z = [dev(y, zp[d], c, b) for d in range(Z)]
    to_b = [
        dev(y, z, other if k % 2 else c, lax.rem(b + k // 2, B)) for k in range(2 * B)
    ]
    peers = to_y[1:] + to_z[1:] + to_b[1:]

    barrier = pltpu.get_barrier_semaphore()
    for to in peers:
        pl.semaphore_signal(barrier, inc=1, device_id=to, device_id_type=MESH)

    loads = [
        [
            (
                pltpu.make_async_copy(l_hbm.at[t, s], lbuf.at[t, s], load_sem.at[0, t, s]),
                pltpu.make_async_copy(r_hbm.at[t, s], rbuf.at[t, s], load_sem.at[1, t, s]),
            )
            for t in range(TERMS)
        ]
        for s in range(SECT)
    ]
    row_ids = o * ROWS + lax.broadcasted_iota(jnp.int32, (ROWS, CAP), 0)
    col_ids = lax.broadcasted_iota(jnp.int32, (ROWS, CAP), 1)
    for copy in small:
        copy.wait()
    masks = []
    me = y * other + z * c
    for s in range(SECT):
        masks.append(((row_ids < ld_ref[s]) & (col_ids < rd_ref[s])).astype(F32))
        for i in range(ROWS):
            own[s, i : i + 1, :] = wave_ref[i, s : s + 1, :]
        own[s] = own[s] * masks[s]
        near[me, s] = own[s]

    pl.semaphore_wait(barrier, len(peers))

    class Path:
        pass

    one, two = Path(), Path()
    one.light, one.heavy, one.light_m, one.heavy_m = to_y, to_z, ym, zm
    one.light_p, one.heavy_p = yp, zp
    one.light_me, one.heavy_me = y, z
    one.g, one.s, one.t, one.u, one.f_s, one.f_r = ga, sa, ta, ua, fa_s, fa_r
    two.light, two.heavy, two.light_m, two.heavy_m = to_z, to_y, zm, ym
    two.light_p, two.heavy_p = zp, yp
    two.light_me, two.heavy_me = z, y
    two.g, two.s, two.t, two.u, two.f_s, two.f_r = gb, sb, tb, ub, fb_s, fb_r
    for p, o_ in ((one, two), (two, one)):
        p.other = o_
        p.n, p.m = len(p.light), len(p.heavy)
        p.near_first = sorted(range(1, p.m), key=lambda d: min(d, p.m - d))
        p.far_first = p.near_first[::-1]

    def both(step, *args):
        @pl.when(c == 0)
        def _():
            step(one, *args)

        @pl.when(c == 1)
        def _():
            step(two, *args)

    def go(copy):
        copy.start()

    def gather_start(p):
        slot = near.at[p.light_me]
        for d in range(1, p.n):
            go(remote(slot, slot, li_s.at[d], li_r.at[d], p.light[d]))

    def gather_heavy(p):
        for d in range(1, p.n):
            slot = near.at[p.light_m[d]]
            remote(slot, slot, li_s.at[d], li_r.at[d], p.light[d]).wait_recv()
        for s in range(SECT):
            for k in range(p.n):
                p.g[s, p.heavy_me, k * ROWS : (k + 1) * ROWS, :] = near[k, s]
            slot = p.g.at[s, p.heavy_me]
            for d in p.far_first:
                go(remote(slot, slot, hi_s.at[s, d], hi_r.at[s, d], p.heavy[d]))
            go(remote(slot, slot, p.f_s.at[s, 0], p.f_r.at[s, 0], partner))

    def gather_forward(p, s):
        for d in p.near_first:
            slot = p.g.at[s, p.heavy_m[d]]
            remote(slot, slot, hi_s.at[s, d], hi_r.at[s, d], p.heavy[d]).wait_recv()
            go(remote(slot, slot, p.f_s.at[s, d], p.f_r.at[s, d], partner))

    def gather_finish(p, s):
        p = p.other
        for d in range(p.m):
            slot = p.g.at[s, p.heavy_m[d]]
            remote(slot, slot, p.f_s.at[s, d], p.f_r.at[s, d], partner).wait_recv()

    def prepare(s):
        for t in range(TERMS):
            loads[s][t][0].wait()
            high, low = split(lbuf[t, s])
            rows = pl.ds(t * CAP, CAP)
            la[s, rows, 0:CAP] = high
            la[s, rows, CAP : 2 * CAP] = high
            la[s, rows, 2 * CAP : 3 * CAP] = low
        for t in range(TERMS):
            loads[s][t][1].wait()
            high, low = split(jnp.transpose(rbuf[t, s]))
            at = 3 * CAP * t
            rb[s, at : at + CAP, :] = high
            rb[s, at + CAP : at + 2 * CAP, :] = low
            rb[s, at + 2 * CAP : at + 3 * CAP, :] = high

    def unpack(s):
        for g in range(Y * Z // 4):
            yy = g // 2
            parts = []
            for zz in range(4 * (g % 2), 4 * (g % 2) + 4):
                parts.append(ga[s, zz, yy * ROWS : (yy + 1) * ROWS, :])
                parts.append(gb[s, yy, zz * ROWS : (zz + 1) * ROWS, :])
            block = jnp.concatenate(parts, axis=0)
            at, n = g * 8 * ROWS, 8 * ROWS
            psi[s, at : at + n, :] = block
            high, low = split(block)
            pb[s, at : at + n, :] = high
            pb[s, CAP + at : CAP + at + n, :] = low
            pb[s, 2 * CAP + at : 2 * CAP + at + n, :] = high

    def first_product(s):
        inner = jnp.dot(la[s], pb[s], preferred_element_type=F32)
        for t in range(TERMS):
            high, low = split(inner[t * CAP : (t + 1) * CAP])
            at = 3 * CAP * t
            ra[s, :, at : at + CAP] = high
            ra[s, :, at + CAP : at + 2 * CAP] = high
            ra[s, :, at + 2 * CAP : at + 3 * CAP] = low

    def second_product(s):
        sig[s] = jnp.dot(ra[s], rb[s], preferred_element_type=F32)

    def pack(s):
        for g in range(Y * Z // 2):
            yy = g // 4
            at, n = g * 4 * ROWS, 4 * ROWS
            block = sig[s, at : at + n, :]
            for k in range(4):
                zz, cc = 2 * (g % 4) + k // 2, k % 2
                part = block[k * ROWS : (k + 1) * ROWS]
                if cc == 0:
                    sa[s, zz, yy * ROWS : (yy + 1) * ROWS, :] = part
                else:
                    sb[s, yy, zz * ROWS : (zz + 1) * ROWS, :] = part

    def core_start(p, s):
        r = p.other
        go(remote(r.s.at[s], r.t.at[s], co_s.at[s], co_r.at[s], partner))

    def correlate(s):
        def body(i, total):
            rows = pl.ds(pl.multiple_of(i * 16, 16), 16)
            pair = sig[s, rows, :] * psi[s, rows, :]
            for i in (0, 8):
                for j in range(0, CAP, 128):
                    total = total + pair[i : i + 8, j : j + 128]
            return total

        return lax.fori_loop(0, CAP // 16, body, jnp.zeros((8, 128), F32))

    def gather_sent(p):
        for d in range(1, p.n):
            remote(near.at[0], near.at[0], li_s.at[d], li_r.at[d], partner).wait_send()
        for s in range(SECT):
            slot = p.g.at[s, 0]
            for d in range(p.m):
                remote(slot, slot, p.f_s.at[s, d], p.f_r.at[s, d], partner).wait_send()
            for d in range(1, p.m):
                remote(slot, slot, hi_s.at[s, d], hi_r.at[s, d], partner).wait_send()

    def scatter_sent(p):
        r = p.other
        for s in range(SECT):
            for d in range(1, p.m):
                remote(p.s.at[s, 0], p.u.at[s, d], ho_s.at[s, d], ho_r.at[s, d], partner).wait_send()
            remote(r.s.at[s], r.t.at[s], co_s.at[s], co_r.at[s], partner).wait_send()

    def scatter_start(p, s):
        remote(p.s.at[s], p.t.at[s], co_s.at[s], co_r.at[s], partner).wait_recv()
        for d in p.far_first + [0]:
            at = p.heavy_p[d]
            p.s[s, at] = p.s[s, at] + p.t[s, at]
            if d:
                go(remote(p.s.at[s, at], p.u.at[s, d], ho_s.at[s, d], ho_r.at[s, d], p.heavy[d]))

    def scalars_start(p):
        for d in p.far_first:
            go(remote(qh.at[0], qh.at[d], qh_s.at[0], qh_r.at[0], p.heavy[d]))

    def scatter_sum(p, s):
        total = p.s[s, p.heavy_me]
        for d in p.near_first:
            remote(p.s.at[s, 0], p.u.at[s, d], ho_s.at[s, d], ho_r.at[s, d], p.heavy[d]).wait_recv()
            total = total + p.u[s, d]
        for k in range(p.n):
            vl[k, s] = total[k * ROWS : (k + 1) * ROWS]

    def scatter_finish(p):
        order = sorted(range(1, p.n), key=lambda d: -min(d, p.n - d))
        for d in order:
            go(remote(vl.at[p.light_p[d]], wl.at[d], lo_s.at[d], lo_r.at[d], p.light[d]))
        total = qh[0]
        rest = qh.at[pl.ds(1, p.m - 1)]
        remote(rest, rest, qh_s.at[0], qh_r.at[0], partner).wait()
        for d in range(1, p.m):
            total = total + qh[d]
        ql[0] = total
        for d in order:
            go(remote(ql.at[0], ql.at[d], ql_s.at[0], ql_r.at[0], p.light[d]))
        scatter_sent(p)
        out = vl[p.light_me]
        for d in order[::-1]:
            remote(vl.at[0], wl.at[d], lo_s.at[d], lo_r.at[d], p.light[d]).wait()
            out = out + wl[d]
        fin[...] = out
        rest = ql.at[pl.ds(1, p.n - 1)]
        remote(rest, rest, ql_s.at[0], ql_r.at[0], partner).wait()
        for d in range(1, p.n):
            total = total + ql[d]
        q[...] = total

    both(gather_start)
    for s in range(SECT):
        for t in range(TERMS):
            loads[s][t][0].start()
            loads[s][t][1].start()
    square = own[0] * own[0] + own[1] * own[1]
    square = sum(square[:, k : k + 128] for k in range(0, CAP, 128))
    q[1:2, :] = jnp.sum(square, axis=0, keepdims=True)
    for s in range(SECT):
        for i in range(ROWS):
            mask_ref[i, s : s + 1, :] = masks[s][i : i + 1]
    both(gather_heavy)
    for s in range(SECT):
        prepare(s)
    both(gather_forward, 0)
    both(gather_finish, 0)
    unpack(0)
    first_product(0)
    both(gather_forward, 1)
    second_product(0)
    pack(0)
    both(core_start, 0)
    both(gather_finish, 1)
    unpack(1)
    first_product(1)
    both(scatter_start, 0)
    first = correlate(0)
    second_product(1)
    q[0:1, :] = jnp.sum(first + correlate(1), axis=0, keepdims=True)
    for k in range(1, 2 * B):
        go(remote(q, qb.at[k], qb_s.at[0], qb_r.at[0], to_b[k]))
    pack(1)
    both(core_start, 1)
    both(scatter_start, 1)
    both(gather_sent)
    rest = qb.at[pl.ds(1, 2 * B - 1)]
    remote(rest, rest, qb_s.at[0], qb_r.at[0], partner).wait()
    total = q[...]
    for k in range(1, 2 * B):
        total = total + qb[k]
    qh[0] = total
    both(scalars_start)
    both(scatter_sum, 0)
    both(scatter_sum, 1)
    both(scatter_finish)

    theta = jnp.sum(q[0:1, :], axis=1, keepdims=True) / jnp.sum(q[1:2, :], axis=1, keepdims=True)
    for s in range(SECT):
        for i in range(ROWS):
            raw_ref[i, s : s + 1, :] = fin[s, i : i + 1]
            shift_ref[i, s : s + 1, :] = theta * own[s, i : i + 1]

def local(wave, left_op, right_op, left_dims, right_dims):
    dma = pltpu.SemaphoreType.DMA
    chunk = (ROWS, CAP)
    vmem = pltpu.VMEM
    raw, mask, shift = pl.pallas_call(
        kernel,
        out_shape=[jax.ShapeDtypeStruct((ROWS, SECT, CAP), F32)] * 3,
        in_specs=[pl.BlockSpec(memory_space=pltpu.HBM)] * 5,
        out_specs=[pl.BlockSpec(memory_space=vmem)] * 3,
        scratch_shapes=[
            pltpu.SMEM((SECT,), jnp.int32),
            pltpu.SMEM((SECT,), jnp.int32),
            vmem((ROWS, SECT, CAP), F32),
            dma((3,)),
            vmem((TERMS, SECT, CAP, CAP), F32),
            vmem((TERMS, SECT, CAP, CAP), F32),
            dma((2, TERMS, SECT)),
            vmem((SECT,) + chunk, F32),
            vmem((Z, SECT) + chunk, F32),
            vmem((SECT, Z, Y * ROWS, CAP), F32),
            vmem((SECT, Y, Z * ROWS, CAP), F32),
            vmem((SECT, CAP, CAP), F32),
            vmem((SECT, TERMS * CAP, 3 * CAP), BF),
            vmem((SECT, 3 * CAP, CAP), BF),
            vmem((SECT, CAP, 3 * TERMS * CAP), BF),
            vmem((SECT, 3 * TERMS * CAP, CAP), BF),
            vmem((SECT, CAP, CAP), F32),
        ]
        + [vmem((SECT, Z, Y * ROWS, CAP), F32), vmem((SECT, Y, Z * ROWS, CAP), F32)] * 3
        + [
            vmem((Z, SECT) + chunk, F32),
            vmem((Z, SECT) + chunk, F32),
            vmem((SECT,) + chunk, F32),
            vmem((2, 128), F32),
            vmem((2 * B, 2, 128), F32),
            vmem((Z, 2, 128), F32),
            vmem((Z, 2, 128), F32),
        ]
        + [dma((Z,))] * 2
        + [dma((SECT, Z))] * 6
        + [dma((SECT,))] * 2
        + [dma((SECT, Z))] * 2
        + [dma((Z,))] * 2
        + [dma((1,))] * 6,
        compiler_params=pltpu.CompilerParams(
            collective_id=0, has_side_effects=True, vmem_limit_bytes=64 * 1024 * 1024
        ),
        cost_estimate=pl.CostEstimate(
            flops=6_000_000_000, bytes_accessed=5_000_000, transcendentals=0
        ),
    )(left_dims, right_dims, wave, left_op, right_op)
    sigma = raw * mask
    return sigma, sigma - shift


def solution(mesh):
    in_specs = (
        P("ops", "blk", None),
        P("ops", "blk", None, None),
        P("ops", "blk", None, None),
        P("blk"),
        P("blk"),
    )
    out_specs = (P("ops", "blk", None), P("ops", "blk", None))
    return jax.shard_map(local, mesh=mesh, in_specs=in_specs, out_specs=out_specs, check_vma=False)
```

```python
import jax
import jax.numpy as jnp
from jax import lax
from jax.experimental import pallas as pl
from jax.experimental.pallas import tpu as pltpu
from jax.sharding import PartitionSpec as P

Y, Z, C, B = 4, 8, 2, 8
ROWS = 6
CAP = 384
TERMS, SECT = 2, 2
MESH = pl.DeviceIdType.MESH
BF, F32 = jnp.bfloat16, jnp.float32


def split(x):
    high = x.astype(BF)
    return high, (x - high.astype(F32)).astype(BF)


def kernel(
    ld_hbm, rd_hbm, wave_hbm, l_hbm, r_hbm, raw_ref, mask_ref, shift_ref,
    ld_ref, rd_ref, in_sem,
    lbuf, rbuf, load_sem,
    own, near, ga, gb, psi, la, pb, ra, rb, sig,
    sa, sb, ta, tb, ua, ub, vl, wl, fin,
    q, qb, qh, ql,
    li_s, li_r, hi_s, hi_r, fa_s, fa_r, fb_s, fb_r,
    co_s, co_r, ho_s, ho_r, lo_s, lo_r,
    qb_s, qb_r, qh_s, qh_r, ql_s, ql_r,
):
    o, b = lax.axis_index("ops"), lax.axis_index("blk")
    y, z, c = o // (Z * C), lax.rem(o // C, Z), lax.rem(o, C)
    other = 1 - c
    me = y * other + z * c

    small = [
        pltpu.make_async_copy(wave_hbm, near.at[me], in_sem.at[0]),
        pltpu.make_async_copy(ld_hbm, ld_ref, in_sem.at[1]),
        pltpu.make_async_copy(rd_hbm, rd_ref, in_sem.at[2]),
    ]
    for copy in small:
        copy.start()

    yp = [lax.rem(y + d, Y) for d in range(Y)]
    ym = [lax.rem(y - d + Y, Y) for d in range(Y)]
    zp = [lax.rem(z + d, Z) for d in range(Z)]
    zm = [lax.rem(z - d + Z, Z) for d in range(Z)]

    def dev(yy, zz, cc, bb):
        return (yy * (Z * C) + zz * C + cc, bb)

    def remote(src, dst, send, recv, to):
        return pltpu.make_async_remote_copy(
            src_ref=src, dst_ref=dst, send_sem=send, recv_sem=recv,
            device_id=to, device_id_type=MESH,
        )

    partner = dev(y, z, other, b)
    to_y = [dev(yp[d], z, c, b) for d in range(Y)]
    to_z = [dev(y, zp[d], c, b) for d in range(Z)]
    to_b = [
        dev(y, z, other if k % 2 else c, lax.rem(b + k // 2, B)) for k in range(2 * B)
    ]
    peers = to_y[1:] + to_z[1:] + to_b[1:]

    barrier = pltpu.get_barrier_semaphore()
    for to in peers:
        pl.semaphore_signal(barrier, inc=1, device_id=to, device_id_type=MESH)

    loads = [
        [
            (
                pltpu.make_async_copy(l_hbm.at[t, s], lbuf.at[t, s], load_sem.at[0, t, s]),
                pltpu.make_async_copy(r_hbm.at[t, s], rbuf.at[t, s], load_sem.at[1, t, s]),
            )
            for t in range(TERMS)
        ]
        for s in range(SECT)
    ]
    pl.semaphore_wait(barrier, len(peers))

    class Path:
        pass

    one, two = Path(), Path()
    one.row, one.gap = (z * C + c) * ROWS, (Z * C - 1) * ROWS
    two.row, two.gap = (y * Z * C + c) * ROWS, (C - 1) * ROWS
    one.light, one.heavy, one.light_m, one.heavy_m = to_y, to_z, ym, zm
    one.light_p, one.heavy_p = yp, zp
    one.light_me, one.heavy_me = y, z
    one.g, one.s, one.t, one.u, one.f_s, one.f_r = ga, sa, ta, ua, fa_s, fa_r
    two.light, two.heavy, two.light_m, two.heavy_m = to_z, to_y, zm, ym
    two.light_p, two.heavy_p = zp, yp
    two.light_me, two.heavy_me = z, y
    two.g, two.s, two.t, two.u, two.f_s, two.f_r = gb, sb, tb, ub, fb_s, fb_r
    for p, o_ in ((one, two), (two, one)):
        p.other = o_
        p.n, p.m = len(p.light), len(p.heavy)
        p.near_first = sorted(range(1, p.m), key=lambda d: min(d, p.m - d))
        p.far_first = p.near_first[::-1]

    def both(step, *args):
        @pl.when(c == 0)
        def _():
            step(one, *args)

        @pl.when(c == 1)
        def _():
            step(two, *args)

    def go(copy):
        copy.start()

    def gather_start(p):
        for d in range(1, p.n):
            go(remote(wave_hbm, near.at[p.light_me], li_s.at[d], li_r.at[d], p.light[d]))

    def gather_heavy(p):
        for d in range(1, p.n):
            slot = near.at[p.light_m[d]]
            remote(slot, slot, li_s.at[d], li_r.at[d], p.light[d]).wait_recv()
        size = (p.n * ROWS, CAP)
        at, row = lax.broadcasted_iota(jnp.int32, size, 0), p.row
        row = row + at + sum((at >= k * ROWS).astype(jnp.int32) for k in range(1, p.n)) * p.gap
        col = lax.broadcasted_iota(jnp.int32, size, 1)
        for s in range(SECT):
            for k in range(p.n):
                for i in range(ROWS):
                    p.g[s, p.heavy_me, k * ROWS + i : k * ROWS + i + 1, :] = near[k, i, s : s + 1, :]
            inside = (row < ld_ref[s]) & (col < rd_ref[s])
            p.g[s, p.heavy_me] = jnp.where(inside, p.g[s, p.heavy_me], 0.0)

    def gather_bundle(p, s):
        slot = p.g.at[s, p.heavy_me]
        for d in p.far_first:
            go(remote(slot, slot, hi_s.at[s, d], hi_r.at[s, d], p.heavy[d]))
        go(remote(slot, slot, p.f_s.at[s, 0], p.f_r.at[s, 0], partner))

    def gather_forward(p, s):
        for d in p.near_first:
            slot = p.g.at[s, p.heavy_m[d]]
            remote(slot, slot, hi_s.at[s, d], hi_r.at[s, d], p.heavy[d]).wait_recv()
            go(remote(slot, slot, p.f_s.at[s, d], p.f_r.at[s, d], partner))

    def gather_finish(p, s):
        p = p.other
        for d in range(p.m):
            slot = p.g.at[s, p.heavy_m[d]]
            remote(slot, slot, p.f_s.at[s, d], p.f_r.at[s, d], partner).wait_recv()

    def prepare(s):
        for t in range(TERMS):
            loads[s][t][0].wait()
            high, low = split(lbuf[t, s])
            rows = pl.ds(t * CAP, CAP)
            la[s, rows, 0:CAP] = high
            la[s, rows, CAP : 2 * CAP] = high
            la[s, rows, 2 * CAP : 3 * CAP] = low
        for t in range(TERMS):
            loads[s][t][1].wait()
            high, low = split(jnp.transpose(rbuf[t, s]))
            at = 3 * CAP * t
            rb[s, at : at + CAP, :] = high
            rb[s, at + CAP : at + 2 * CAP, :] = low
            rb[s, at + 2 * CAP : at + 3 * CAP, :] = high

    def unpack(s):
        for g in range(Y * Z // 4):
            yy = g // 2
            parts = []
            for zz in range(4 * (g % 2), 4 * (g % 2) + 4):
                parts.append(ga[s, zz, yy * ROWS : (yy + 1) * ROWS, :])
                parts.append(gb[s, yy, zz * ROWS : (zz + 1) * ROWS, :])
            block = jnp.concatenate(parts, axis=0)
            at, n = g * 8 * ROWS, 8 * ROWS
            psi[s, at : at + n, :] = block
            high, low = split(block)
            pb[s, at : at + n, :] = high
            pb[s, CAP + at : CAP + at + n, :] = low
            pb[s, 2 * CAP + at : 2 * CAP + at + n, :] = high

    def first_product(s):
        inner = jnp.dot(la[s], pb[s], preferred_element_type=F32)
        for t in range(TERMS):
            high, low = split(inner[t * CAP : (t + 1) * CAP])
            at = 3 * CAP * t
            ra[s, :, at : at + CAP] = high
            ra[s, :, at + CAP : at + 2 * CAP] = high
            ra[s, :, at + 2 * CAP : at + 3 * CAP] = low

    def second_product(s):
        sig[s] = jnp.dot(ra[s], rb[s], preferred_element_type=F32)

    def pack(s):
        for g in range(Y * Z // 2):
            yy = g // 4
            at, n = g * 4 * ROWS, 4 * ROWS
            block = sig[s, at : at + n, :]
            for k in range(4):
                zz, cc = 2 * (g % 4) + k // 2, k % 2
                part = block[k * ROWS : (k + 1) * ROWS]
                if cc == 0:
                    sa[s, zz, yy * ROWS : (yy + 1) * ROWS, :] = part
                else:
                    sb[s, yy, zz * ROWS : (zz + 1) * ROWS, :] = part

    def core_start(p, s):
        r = p.other
        go(remote(r.s.at[s], r.t.at[s], co_s.at[s], co_r.at[s], partner))

    def correlate(s):
        def body(i, total):
            rows = pl.ds(pl.multiple_of(i * 16, 16), 16)
            pair = sig[s, rows, :] * psi[s, rows, :]
            for i in (0, 8):
                for j in range(0, CAP, 128):
                    total = total + pair[i : i + 8, j : j + 128]
            return total

        return lax.fori_loop(0, CAP // 16, body, jnp.zeros((8, 128), F32))

    def gather_sent(p):
        for d in range(1, p.n):
            remote(wave_hbm, near.at[0], li_s.at[d], li_r.at[d], partner).wait_send()
        for s in range(SECT):
            slot = p.g.at[s, 0]
            for d in range(p.m):
                remote(slot, slot, p.f_s.at[s, d], p.f_r.at[s, d], partner).wait_send()
            for d in range(1, p.m):
                remote(slot, slot, hi_s.at[s, d], hi_r.at[s, d], partner).wait_send()

    def scatter_sent(p):
        r = p.other
        for s in range(SECT):
            for d in range(1, p.m):
                remote(p.s.at[s, 0], p.u.at[s, d], ho_s.at[s, d], ho_r.at[s, d], partner).wait_send()
            remote(r.s.at[s], r.t.at[s], co_s.at[s], co_r.at[s], partner).wait_send()

    def scatter_start(p, s):
        remote(p.s.at[s], p.t.at[s], co_s.at[s], co_r.at[s], partner).wait_recv()
        for d in p.far_first + [0]:
            at = p.heavy_p[d]
            p.s[s, at] = p.s[s, at] + p.t[s, at]
            if d:
                go(remote(p.s.at[s, at], p.u.at[s, d], ho_s.at[s, d], ho_r.at[s, d], p.heavy[d]))

    def scalars_start(p):
        for d in p.far_first:
            go(remote(qh.at[0], qh.at[d], qh_s.at[0], qh_r.at[0], p.heavy[d]))

    def scatter_sum(p, s):
        total = p.s[s, p.heavy_me]
        for d in p.near_first:
            remote(p.s.at[s, 0], p.u.at[s, d], ho_s.at[s, d], ho_r.at[s, d], p.heavy[d]).wait_recv()
            total = total + p.u[s, d]
        for k in range(p.n):
            vl[k, s] = total[k * ROWS : (k + 1) * ROWS]

    def scatter_finish(p):
        order = sorted(range(1, p.n), key=lambda d: -min(d, p.n - d))
        for d in order:
            go(remote(vl.at[p.light_p[d]], wl.at[d], lo_s.at[d], lo_r.at[d], p.light[d]))
        total = qh[0]
        rest = qh.at[pl.ds(1, p.m - 1)]
        remote(rest, rest, qh_s.at[0], qh_r.at[0], partner).wait()
        for d in range(1, p.m):
            total = total + qh[d]
        ql[0] = total
        for d in order:
            go(remote(ql.at[0], ql.at[d], ql_s.at[0], ql_r.at[0], p.light[d]))
        scatter_sent(p)
        out = vl[p.light_me]
        for d in order[::-1]:
            remote(vl.at[0], wl.at[d], lo_s.at[d], lo_r.at[d], p.light[d]).wait()
            out = out + wl[d]
        fin[...] = out
        rest = ql.at[pl.ds(1, p.n - 1)]
        remote(rest, rest, ql_s.at[0], ql_r.at[0], partner).wait()
        for d in range(1, p.n):
            total = total + ql[d]
        q[...] = total

    both(gather_start)
    for s in range(SECT):
        for t in range(TERMS):
            loads[s][t][0].start()
            loads[s][t][1].start()
    row_ids = o * ROWS + lax.broadcasted_iota(jnp.int32, (ROWS, CAP), 0)
    col_ids = lax.broadcasted_iota(jnp.int32, (ROWS, CAP), 1)
    for copy in small:
        copy.wait()
    masks = []
    for s in range(SECT):
        masks.append(((row_ids < ld_ref[s]) & (col_ids < rd_ref[s])).astype(F32))
        for i in range(ROWS):
            own[s, i : i + 1, :] = near[me, i, s : s + 1, :]
        own[s] = own[s] * masks[s]
    square = own[0] * own[0] + own[1] * own[1]
    square = sum(square[:, k : k + 128] for k in range(0, CAP, 128))
    q[1:2, :] = jnp.sum(square, axis=0, keepdims=True)
    for s in range(SECT):
        for i in range(ROWS):
            mask_ref[i, s : s + 1, :] = masks[s][i : i + 1]
    both(gather_heavy)
    both(gather_bundle, 0)
    prepare(0)
    both(gather_bundle, 1)
    prepare(1)
    both(gather_forward, 0)
    both(gather_finish, 0)
    unpack(0)
    first_product(0)
    both(gather_forward, 1)
    second_product(0)
    pack(0)
    both(core_start, 0)
    both(gather_finish, 1)
    unpack(1)
    first_product(1)
    both(scatter_start, 0)
    first = correlate(0)
    second_product(1)
    q[0:1, :] = jnp.sum(first + correlate(1), axis=0, keepdims=True)
    for k in range(1, 2 * B):
        go(remote(q, qb.at[k], qb_s.at[0], qb_r.at[0], to_b[k]))
    pack(1)
    both(core_start, 1)
    both(scatter_start, 1)
    both(gather_sent)
    rest = qb.at[pl.ds(1, 2 * B - 1)]
    remote(rest, rest, qb_s.at[0], qb_r.at[0], partner).wait()
    total = q[...]
    for k in range(1, 2 * B):
        total = total + qb[k]
    qh[0] = total
    both(scalars_start)
    both(scatter_sum, 0)
    both(scatter_sum, 1)
    both(scatter_finish)

    theta = jnp.sum(q[0:1, :], axis=1, keepdims=True) / jnp.sum(q[1:2, :], axis=1, keepdims=True)
    for s in range(SECT):
        for i in range(ROWS):
            raw_ref[i, s : s + 1, :] = fin[s, i : i + 1]
            shift_ref[i, s : s + 1, :] = theta * own[s, i : i + 1]

def local(wave, left_op, right_op, left_dims, right_dims):
    dma = pltpu.SemaphoreType.DMA
    chunk = (ROWS, CAP)
    vmem = pltpu.VMEM
    raw, mask, shift = pl.pallas_call(
        kernel,
        out_shape=[jax.ShapeDtypeStruct((ROWS, SECT, CAP), F32)] * 3,
        in_specs=[pl.BlockSpec(memory_space=pltpu.HBM)] * 5,
        out_specs=[pl.BlockSpec(memory_space=vmem)] * 3,
        scratch_shapes=[
            pltpu.SMEM((SECT,), jnp.int32),
            pltpu.SMEM((SECT,), jnp.int32),
            dma((3,)),
            vmem((TERMS, SECT, CAP, CAP), F32),
            vmem((TERMS, SECT, CAP, CAP), F32),
            dma((2, TERMS, SECT)),
            vmem((SECT,) + chunk, F32),
            vmem((Z, ROWS, SECT, CAP), F32),
            vmem((SECT, Z, Y * ROWS, CAP), F32),
            vmem((SECT, Y, Z * ROWS, CAP), F32),
            vmem((SECT, CAP, CAP), F32),
            vmem((SECT, TERMS * CAP, 3 * CAP), BF),
            vmem((SECT, 3 * CAP, CAP), BF),
            vmem((SECT, CAP, 3 * TERMS * CAP), BF),
            vmem((SECT, 3 * TERMS * CAP, CAP), BF),
            vmem((SECT, CAP, CAP), F32),
        ]
        + [vmem((SECT, Z, Y * ROWS, CAP), F32), vmem((SECT, Y, Z * ROWS, CAP), F32)] * 3
        + [
            vmem((Z, SECT) + chunk, F32),
            vmem((Z, SECT) + chunk, F32),
            vmem((SECT,) + chunk, F32),
            vmem((2, 128), F32),
            vmem((2 * B, 2, 128), F32),
            vmem((Z, 2, 128), F32),
            vmem((Z, 2, 128), F32),
        ]
        + [dma((Z,))] * 2
        + [dma((SECT, Z))] * 6
        + [dma((SECT,))] * 2
        + [dma((SECT, Z))] * 2
        + [dma((Z,))] * 2
        + [dma((1,))] * 6,
        compiler_params=pltpu.CompilerParams(
            collective_id=0, has_side_effects=True, vmem_limit_bytes=64 * 1024 * 1024
        ),
        cost_estimate=pl.CostEstimate(
            flops=6_000_000_000, bytes_accessed=5_000_000, transcendentals=0
        ),
    )(left_dims, right_dims, wave, left_op, right_op)
    sigma = raw * mask
    return sigma, sigma - shift


def solution(mesh):
    in_specs = (
        P("ops", "blk", None),
        P("ops", "blk", None, None),
        P("ops", "blk", None, None),
        P("blk"),
        P("blk"),
    )
    out_specs = (P("ops", "blk", None), P("ops", "blk", None))
    return jax.shard_map(local, mesh=mesh, in_specs=in_specs, out_specs=out_specs, check_vma=False)
```

```python
import jax
import jax.numpy as jnp
from jax import lax
from jax.experimental import pallas as pl
from jax.experimental.pallas import tpu as pltpu
from jax.sharding import PartitionSpec as P

Y, Z, C, B = 4, 8, 2, 8
ROWS = 6
CAP = 384
TERMS, SECT = 2, 2
MESH = pl.DeviceIdType.MESH
BF, F32 = jnp.bfloat16, jnp.float32


def split(x):
    high = x.astype(BF)
    return high, (x - high.astype(F32)).astype(BF)


def kernel(
    ld_hbm, rd_hbm, wave_hbm, l_hbm, r_hbm, raw_ref, mask_ref, shift_ref,
    ld_ref, rd_ref, in_sem,
    lbuf, rbuf, load_sem,
    own, near, ga, gb, psi, la, pb, ra, rb, sig,
    sa, sb, ta, tb, ua, ub, vl, wl,
    q, qb, qh, ql,
    li_s, li_r, hi_s, hi_r, fa_s, fa_r, fb_s, fb_r,
    co_s, co_r, ho_s, ho_r, lo_s, lo_r,
    qb_s, qb_r, qh_s, qh_r, ql_s, ql_r,
):
    o, b = lax.axis_index("ops"), lax.axis_index("blk")
    y, z, c = o // (Z * C), lax.rem(o // C, Z), lax.rem(o, C)
    other = 1 - c
    me = y * other + z * c

    small = [
        pltpu.make_async_copy(wave_hbm, near.at[me], in_sem.at[0]),
        pltpu.make_async_copy(ld_hbm, ld_ref, in_sem.at[1]),
        pltpu.make_async_copy(rd_hbm, rd_ref, in_sem.at[2]),
    ]
    for copy in small:
        copy.start()

    yp = [lax.rem(y + d, Y) for d in range(Y)]
    ym = [lax.rem(y - d + Y, Y) for d in range(Y)]
    zp = [lax.rem(z + d, Z) for d in range(Z)]
    zm = [lax.rem(z - d + Z, Z) for d in range(Z)]

    def dev(yy, zz, cc, bb):
        return (yy * (Z * C) + zz * C + cc, bb)

    def remote(src, dst, send, recv, to):
        return pltpu.make_async_remote_copy(
            src_ref=src, dst_ref=dst, send_sem=send, recv_sem=recv,
            device_id=to, device_id_type=MESH,
        )

    partner = dev(y, z, other, b)
    to_y = [dev(yp[d], z, c, b) for d in range(Y)]
    to_z = [dev(y, zp[d], c, b) for d in range(Z)]
    to_b = [
        dev(y, z, other if k % 2 else c, lax.rem(b + k // 2, B)) for k in range(2 * B)
    ]
    peers = [to_z[4], to_y[2], to_z[3], to_z[5]] + to_b[8:12] + to_b[4:8] + to_b[12:]
    peers += [to_y[1], to_y[3], to_z[2], to_z[6]] + to_b[2:4] + [to_z[1], to_z[7], to_b[1]]

    barrier = pltpu.get_barrier_semaphore()
    for to in peers:
        pl.semaphore_signal(barrier, inc=1, device_id=to, device_id_type=MESH)

    loads = [
        [
            (
                pltpu.make_async_copy(l_hbm.at[t, s], lbuf.at[t, s], load_sem.at[0, t, s]),
                pltpu.make_async_copy(r_hbm.at[t, s], rbuf.at[t, s], load_sem.at[1, t, s]),
            )
            for t in range(TERMS)
        ]
        for s in range(SECT)
    ]
    pl.semaphore_wait(barrier, len(peers))

    class Path:
        pass

    one, two = Path(), Path()
    one.row, one.gap = (z * C + c) * ROWS, (Z * C - 1) * ROWS
    two.row, two.gap = (y * Z * C + c) * ROWS, (C - 1) * ROWS
    one.light, one.heavy, one.light_m, one.heavy_m = to_y, to_z, ym, zm
    one.light_p, one.heavy_p = yp, zp
    one.light_me, one.heavy_me = y, z
    one.g, one.s, one.t, one.u, one.f_s, one.f_r = ga, sa, ta, ua, fa_s, fa_r
    two.light, two.heavy, two.light_m, two.heavy_m = to_z, to_y, zm, ym
    two.light_p, two.heavy_p = zp, yp
    two.light_me, two.heavy_me = z, y
    two.g, two.s, two.t, two.u, two.f_s, two.f_r = gb, sb, tb, ub, fb_s, fb_r
    for p, o_ in ((one, two), (two, one)):
        p.other = o_
        p.n, p.m = len(p.light), len(p.heavy)
        p.near_first = sorted(range(1, p.m), key=lambda d: min(d, p.m - d))
        p.far_first = p.near_first[::-1]

    def both(step, *args):
        @pl.when(c == 0)
        def _():
            step(one, *args)

        @pl.when(c == 1)
        def _():
            step(two, *args)

    def go(copy):
        copy.start()

    def gather_start(p):
        for d in range(1, p.n):
            go(remote(wave_hbm, near.at[p.light_me], li_s.at[0], li_r.at[0], p.light[d]))

    def gather_heavy(p):
        rest = near.at[pl.ds(1, p.n - 1)]
        remote(rest, rest, li_s.at[0], li_r.at[0], partner).wait_recv()
        size = (p.n * ROWS, CAP)
        at, row = lax.broadcasted_iota(jnp.int32, size, 0), p.row
        row = row + at + sum((at >= k * ROWS).astype(jnp.int32) for k in range(1, p.n)) * p.gap
        col = lax.broadcasted_iota(jnp.int32, size, 1)
        for s in range(SECT):
            for k in range(p.n):
                for i in range(ROWS):
                    p.g[s, p.heavy_me, k * ROWS + i : k * ROWS + i + 1, :] = near[k, i, s : s + 1, :]
            inside = (row < ld_ref[s]) & (col < rd_ref[s])
            p.g[s, p.heavy_me] = jnp.where(inside, p.g[s, p.heavy_me], 0.0)

    def gather_bundle(p, s):
        slot = p.g.at[s, p.heavy_me]
        for d in p.far_first:
            go(remote(slot, slot, hi_s.at[s], hi_r.at[s], p.heavy[d]))

    def rest_of(buf, s, n):
        return buf.at[s, pl.ds(1, n - 1)]

    def gather_forward(p, s):
        rest = rest_of(p.g, s, p.m)
        remote(rest, rest, hi_s.at[s], hi_r.at[s], partner).wait_recv()
        go(remote(p.g.at[s], p.g.at[s], p.f_s.at[s], p.f_r.at[s], partner))

    def gather_finish(p, s):
        p = p.other
        remote(p.g.at[s], p.g.at[s], p.f_s.at[s], p.f_r.at[s], partner).wait_recv()

    def prepare(s):
        for t in range(TERMS):
            loads[s][t][0].wait()
            high, low = split(lbuf[t, s])
            rows = pl.ds(t * CAP, CAP)
            la[s, rows, 0:CAP] = high
            la[s, rows, CAP : 2 * CAP] = high
            la[s, rows, 2 * CAP : 3 * CAP] = low
        for t in range(TERMS):
            loads[s][t][1].wait()
            high, low = split(jnp.transpose(rbuf[t, s]))
            at = 3 * CAP * t
            rb[s, at : at + CAP, :] = high
            rb[s, at + CAP : at + 2 * CAP, :] = low
            rb[s, at + 2 * CAP : at + 3 * CAP, :] = high

    def unpack(s):
        for g in range(Y * Z // 4):
            yy = g // 2
            parts = []
            for zz in range(4 * (g % 2), 4 * (g % 2) + 4):
                parts.append(ga[s, zz, yy * ROWS : (yy + 1) * ROWS, :])
                parts.append(gb[s, yy, zz * ROWS : (zz + 1) * ROWS, :])
            block = jnp.concatenate(parts, axis=0)
            at, n = g * 8 * ROWS, 8 * ROWS
            psi[s, at : at + n, :] = block
            high, low = split(block)
            pb[s, at : at + n, :] = high
            pb[s, CAP + at : CAP + at + n, :] = low
            pb[s, 2 * CAP + at : 2 * CAP + at + n, :] = high

    def first_product(s):
        inner = jnp.dot(la[s], pb[s], preferred_element_type=F32)
        for t in range(TERMS):
            high, low = split(inner[t * CAP : (t + 1) * CAP])
            at = 3 * CAP * t
            ra[s, :, at : at + CAP] = high
            ra[s, :, at + CAP : at + 2 * CAP] = high
            ra[s, :, at + 2 * CAP : at + 3 * CAP] = low

    def second_product(s):
        sig[s] = jnp.dot(ra[s], rb[s], preferred_element_type=F32)

    def pack(s):
        for g in range(Y * Z // 2):
            yy = g // 4
            at, n = g * 4 * ROWS, 4 * ROWS
            block = sig[s, at : at + n, :]
            for k in range(4):
                zz, cc = 2 * (g % 4) + k // 2, k % 2
                part = block[k * ROWS : (k + 1) * ROWS]
                if cc == 0:
                    sa[s, zz, yy * ROWS : (yy + 1) * ROWS, :] = part
                else:
                    sb[s, yy, zz * ROWS : (zz + 1) * ROWS, :] = part

    def core_start(p, s):
        r = p.other
        go(remote(r.s.at[s], r.t.at[s], co_s.at[s], co_r.at[s], partner))

    def correlate(s):
        def body(i, total):
            rows = pl.ds(pl.multiple_of(i * 16, 16), 16)
            pair = sig[s, rows, :] * psi[s, rows, :]
            for i in (0, 8):
                for j in range(0, CAP, 128):
                    total = total + pair[i : i + 8, j : j + 128]
            return total

        return lax.fori_loop(0, CAP // 16, body, jnp.zeros((8, 128), F32))

    def gather_sent(p):
        rest = near.at[pl.ds(1, p.n - 1)]
        remote(rest, rest, li_s.at[0], li_r.at[0], partner).wait_send()
        for s in range(SECT):
            rest = rest_of(p.g, s, p.m)
            remote(rest, rest, hi_s.at[s], hi_r.at[s], partner).wait_send()
            remote(p.g.at[s], p.g.at[s], p.f_s.at[s], p.f_r.at[s], partner).wait_send()

    def scatter_sent(p):
        r = p.other
        for s in range(SECT):
            rest = rest_of(p.u, s, p.m)
            remote(rest, rest, ho_s.at[s], ho_r.at[s], partner).wait_send()
            remote(r.s.at[s], r.t.at[s], co_s.at[s], co_r.at[s], partner).wait_send()

    def scatter_start(p, s):
        remote(p.s.at[s], p.t.at[s], co_s.at[s], co_r.at[s], partner).wait_recv()
        for d in p.far_first + [0]:
            at = p.heavy_p[d]
            p.s[s, at] = p.s[s, at] + p.t[s, at]
            if d:
                go(remote(p.s.at[s, at], p.u.at[s, d], ho_s.at[s], ho_r.at[s], p.heavy[d]))

    def scalars_start(p):
        for d in p.far_first:
            go(remote(qh.at[0], qh.at[d], qh_s.at[0], qh_r.at[0], p.heavy[d]))

    def scatter_sum(p, s):
        total = p.s[s, p.heavy_me]
        rest = rest_of(p.u, s, p.m)
        remote(rest, rest, ho_s.at[s], ho_r.at[s], partner).wait_recv()
        for d in range(1, p.m):
            total = total + p.u[s, d]
        for k in range(p.n):
            vl[k, s] = total[k * ROWS : (k + 1) * ROWS]

    def scatter_finish(p):
        order = sorted(range(1, p.n), key=lambda d: -min(d, p.n - d))
        for d in order:
            go(remote(vl.at[p.light_p[d]], wl.at[d], lo_s.at[0], lo_r.at[0], p.light[d]))
        total = qh[0]
        rest = qh.at[pl.ds(1, p.m - 1)]
        remote(rest, rest, qh_s.at[0], qh_r.at[0], partner).wait()
        for d in range(1, p.m):
            total = total + qh[d]
        ql[0] = total
        for d in order:
            go(remote(ql.at[0], ql.at[d], ql_s.at[0], ql_r.at[0], p.light[d]))
        gather_sent(p)
        scatter_sent(p)
        out = vl[p.light_me]
        rest = wl.at[pl.ds(1, p.n - 1)]
        remote(rest, rest, lo_s.at[0], lo_r.at[0], partner).wait()
        for d in range(1, p.n):
            out = out + wl[d]
        for s in range(SECT):
            for i in range(ROWS):
                raw_ref[i, s : s + 1, :] = out[s, i : i + 1]
        rest = ql.at[pl.ds(1, p.n - 1)]
        remote(rest, rest, ql_s.at[0], ql_r.at[0], partner).wait()
        for d in range(1, p.n):
            total = total + ql[d]
        q[...] = total

    both(gather_start)
    for s in range(SECT):
        for t in range(TERMS):
            loads[s][t][0].start()
            loads[s][t][1].start()
    row_ids = o * ROWS + lax.broadcasted_iota(jnp.int32, (ROWS, CAP), 0)
    col_ids = lax.broadcasted_iota(jnp.int32, (ROWS, CAP), 1)
    for copy in small:
        copy.wait()
    masks = []
    for s in range(SECT):
        masks.append(((row_ids < ld_ref[s]) & (col_ids < rd_ref[s])).astype(F32))
        for i in range(ROWS):
            own[s, i : i + 1, :] = near[me, i, s : s + 1, :]
        own[s] = own[s] * masks[s]
    square = own[0] * own[0] + own[1] * own[1]
    square = sum(square[:, k : k + 128] for k in range(0, CAP, 128))
    q[1:2, :] = jnp.sum(square, axis=0, keepdims=True)
    for s in range(SECT):
        for i in range(ROWS):
            mask_ref[i, s : s + 1, :] = masks[s][i : i + 1]
    both(gather_heavy)
    both(gather_bundle, 0)
    prepare(0)
    both(gather_bundle, 1)
    prepare(1)
    both(gather_forward, 0)
    both(gather_finish, 0)
    unpack(0)
    first_product(0)
    both(gather_forward, 1)
    second_product(0)
    pack(0)
    both(core_start, 0)
    both(gather_finish, 1)
    unpack(1)
    first_product(1)
    both(scatter_start, 0)
    first = correlate(0)
    second_product(1)
    q[0:1, :] = jnp.sum(first + correlate(1), axis=0, keepdims=True)
    for k in range(1, 2 * B):
        go(remote(q, qb.at[k], qb_s.at[0], qb_r.at[0], to_b[k]))
    pack(1)
    both(core_start, 1)
    both(scatter_start, 1)
    rest = qb.at[pl.ds(1, 2 * B - 1)]
    remote(rest, rest, qb_s.at[0], qb_r.at[0], partner).wait()
    total = q[...]
    for k in range(1, 2 * B):
        total = total + qb[k]
    qh[0] = total
    both(scalars_start)
    both(scatter_sum, 0)
    both(scatter_sum, 1)
    both(scatter_finish)

    theta = jnp.sum(q[0:1, :], axis=1, keepdims=True) / jnp.sum(q[1:2, :], axis=1, keepdims=True)
    for s in range(SECT):
        for i in range(ROWS):
            shift_ref[i, s : s + 1, :] = theta * own[s, i : i + 1]

def local(wave, left_op, right_op, left_dims, right_dims):
    dma = pltpu.SemaphoreType.DMA
    chunk = (ROWS, CAP)
    vmem = pltpu.VMEM
    raw, mask, shift = pl.pallas_call(
        kernel,
        out_shape=[jax.ShapeDtypeStruct((ROWS, SECT, CAP), F32)] * 3,
        in_specs=[pl.BlockSpec(memory_space=pltpu.HBM)] * 5,
        out_specs=[pl.BlockSpec(memory_space=vmem)] * 3,
        scratch_shapes=[
            pltpu.SMEM((SECT,), jnp.int32),
            pltpu.SMEM((SECT,), jnp.int32),
            dma((3,)),
            vmem((TERMS, SECT, CAP, CAP), F32),
            vmem((TERMS, SECT, CAP, CAP), F32),
            dma((2, TERMS, SECT)),
            vmem((SECT,) + chunk, F32),
            vmem((Z, ROWS, SECT, CAP), F32),
            vmem((SECT, Z, Y * ROWS, CAP), F32),
            vmem((SECT, Y, Z * ROWS, CAP), F32),
            vmem((SECT, CAP, CAP), F32),
            vmem((SECT, TERMS * CAP, 3 * CAP), BF),
            vmem((SECT, 3 * CAP, CAP), BF),
            vmem((SECT, CAP, 3 * TERMS * CAP), BF),
            vmem((SECT, 3 * TERMS * CAP, CAP), BF),
            vmem((SECT, CAP, CAP), F32),
        ]
        + [vmem((SECT, Z, Y * ROWS, CAP), F32), vmem((SECT, Y, Z * ROWS, CAP), F32)] * 3
        + [
            vmem((Z, SECT) + chunk, F32),
            vmem((Z, SECT) + chunk, F32),
            vmem((2, 128), F32),
            vmem((2 * B, 2, 128), F32),
            vmem((Z, 2, 128), F32),
            vmem((Z, 2, 128), F32),
        ]
        + [dma((Z,))] * 2
        + [dma((SECT,))] * 10
        + [dma((Z,))] * 2
        + [dma((1,))] * 6,
        compiler_params=pltpu.CompilerParams(
            collective_id=0, has_side_effects=True, vmem_limit_bytes=64 * 1024 * 1024
        ),
        cost_estimate=pl.CostEstimate(
            flops=6_000_000_000, bytes_accessed=5_000_000, transcendentals=0
        ),
    )(left_dims, right_dims, wave, left_op, right_op)
    sigma = raw * mask
    return sigma, sigma - shift


def solution(mesh):
    in_specs = (
        P("ops", "blk", None),
        P("ops", "blk", None, None),
        P("ops", "blk", None, None),
        P("blk"),
        P("blk"),
    )
    out_specs = (P("ops", "blk", None), P("ops", "blk", None))
    return jax.shard_map(local, mesh=mesh, in_specs=in_specs, out_specs=out_specs, check_vma=False)
```
